32 devices in a mesh: row: 4 (over y, x), col: 4 (over z), depth: 2 (over core).
Axes of the slice: x: 2, y: 2, z: 4, core: 2. Of those that a mesh axis runs over, the one named last changes fastest.
Arguments:
- x_blocks: float32 [48, 16, 128, 128], P(('row', 'depth'), 'col'), may hold values from -1.2 to 1.2
- x_cols: int32 [48, 16], P(('row', 'depth'), 'col'), may hold values from 0 to 11, as said below
- c_cols: int32 [48, 16], P(('row', 'depth'), 'col'), may hold values from 0 to 11, as said below
Outputs:
- c_blocks: float32 [48, 16, 128, 128], P(('row', 'depth'), 'col')
The draws below stay inside these ranges and needn't reach their ends.
Inputs may be any that keep to these rules, and one draw needn't show every extreme that they name: `x_cols`: within one block row and column tile the 4 entries are distinct. `c_cols`: within one block row and column tile the 4 entries are distinct.
All inputs are finite; a program needn't handle non-finite values.
Results may differ from the reference program's by a relative error of at most 0.0003.
Values sent between devices are 32-bit elements; how exact they have to be, the bound alone decides.
A program may use at most 128 MiB of HBM per device.

```python
import jax
import jax.numpy as jnp
from jax import lax

BS = 128
SLOTS = 4
OUT_SLOTS = 4
NB = 48
TILE = 12
N_COL = 4


def distinct_columns(key, count):
    scores = jax.random.randint(key, (NB, N_COL, TILE), 0, 1 << 20, dtype=jnp.int32)
    scores = scores * TILE + jnp.arange(TILE, dtype=jnp.int32)
    order = jnp.argsort(scores, axis=-1)[:, :, :count]
    return order.astype(jnp.int32).reshape(NB, N_COL * count)


def draw_x_cols(key, part):
    return distinct_columns(jax.random.fold_in(key, 11), SLOTS)


def draw_c_cols(key, part):
    return distinct_columns(jax.random.fold_in(key, 23), OUT_SLOTS)


def block_levels(rng, extent, cuts, low, high):
    gain, own = 1.0, jax.random.fold_in(rng, 6)
    for dim, shards_of in cuts:
        heights = jnp.exp(jax.random.uniform(jax.random.fold_in(own, dim), (shards_of,), jnp.float32, low / len(cuts), high / len(cuts)))
        gain = gain * jnp.repeat(heights, extent[dim] // shards_of).reshape([-1 if axis == dim else 1 for axis in range(len(extent))])
    return gain


def bell_draw(rng, shape, deviation, bound, shards=(), held_as=jnp.bfloat16):
    array = jax.random.normal(rng, shape, jnp.float32) * deviation
    if len(shards) > 0:
        array = block_levels(rng, shape, shards, -0.22, 0.18) * array
    return jnp.clip(array, min=-bound, max=bound).astype(held_as)


def setup_inputs(seed: int = 0) -> dict:
    key_list = jax.random.split(jax.random.key(seed), 4)
    x_blocks = bell_draw(key_list[0], (NB, N_COL * SLOTS, BS, BS), 0.2, 1.2, ((0, 8), (1, 4)), jnp.float32)
    x_cols = draw_x_cols(jax.random.fold_in(key_list[3], 71), 0)
    c_cols = draw_c_cols(jax.random.fold_in(key_list[3], 71), 0)
    return {"x_blocks": x_blocks, "x_cols": x_cols, "c_cols": c_cols}


def block_product(left_blocks, left_cols, right_blocks, right_cols, out_cols):
    picked = jnp.take(right_blocks, left_cols, axis=0)
    picked_cols = jnp.take(right_cols, left_cols, axis=0)
    partial_prod = jnp.einsum("isab,istbc->istac", left_blocks, picked, precision=lax.Precision.HIGHEST)
    matches = (picked_cols[:, :, :, None] == out_cols[:, None, None, :]).astype(jnp.float32)
    return jnp.einsum("istu,istac->iuac", matches, partial_prod, precision=lax.Precision.HIGHEST)


def reference(x_blocks, x_cols, c_cols):
    blocks = x_blocks.reshape(NB, N_COL, SLOTS, BS, BS)
    columns = x_cols.reshape(NB, N_COL, SLOTS)
    kept = c_cols.reshape(NB, N_COL, OUT_SLOTS)

    def one_tile(column_tile):
        kept_here = lax.dynamic_index_in_dim(kept, column_tile, 1, keepdims=False)
        right_all = lax.dynamic_index_in_dim(blocks, column_tile, 1, keepdims=False)
        right_cols_all = lax.dynamic_index_in_dim(columns, column_tile, 1, keepdims=False)

        def add_panel(inner, accum):
            left_here = lax.dynamic_index_in_dim(blocks, inner, 1, keepdims=False)
            left_cols = lax.dynamic_index_in_dim(columns, inner, 1, keepdims=False)
            start = (inner * TILE).astype(jnp.int32)
            right_here = lax.dynamic_slice_in_dim(right_all, start, TILE, 0)
            right_cols = lax.dynamic_slice_in_dim(right_cols_all, start, TILE, 0)
            return accum + block_product(left_here, left_cols, right_here, right_cols, kept_here)

        initial = jnp.zeros((NB, OUT_SLOTS, BS, BS), jnp.float32)
        return lax.fori_loop(0, N_COL, add_panel, initial)

    result = lax.map(one_tile, jnp.arange(N_COL, dtype=jnp.int32))
    return jnp.transpose(result, (1, 0, 2, 3, 4)).reshape(NB, N_COL * OUT_SLOTS, BS, BS)
```

```python
import functools

import jax
import jax.numpy as jnp
from jax import lax
from jax.experimental import pallas as pl
from jax.experimental.pallas import tpu as pltpu
from jax.sharding import PartitionSpec as P

MESH = pl.DeviceIdType.MESH


def split(value):
    high = value.astype(jnp.bfloat16)
    low = (value - high.astype(jnp.float32)).astype(jnp.bfloat16)
    return high, low


def kernel(
    sizes,
    kept_ref,
    names_ref,
    x_ref,
    out_ref,
    right,
    left,
    right_names,
    left_names,
    right_table,
    left_table,
    right_send,
    right_recv,
    core_send,
    core_recv,
    up_send,
    down_send,
    left_recv,
    rn_send,
    rn_recv,
    ln_send,
    ln_recv,
    local_sem,
):
    n_row, n_col, n_depth = sizes
    rows, slots = x_ref.shape[0], x_ref.shape[1]
    n_right = n_row * n_depth
    r, c, d = lax.axis_index("row"), lax.axis_index("col"), lax.axis_index("depth")
    me = r * n_depth + d

    def right_peer(step):
        other = lax.rem(me + step, n_right)
        return {"row": other // n_depth, "depth": lax.rem(other, n_depth)}

    barrier = pltpu.get_barrier_semaphore()
    for step in range(1, n_right):
        pl.semaphore_signal(barrier, inc=1, device_id=right_peer(step), device_id_type=MESH)
    for step in range(1, n_col):
        pl.semaphore_signal(
            barrier, inc=1, device_id={"col": lax.rem(c + step, n_col)}, device_id_type=MESH
        )
    pl.semaphore_wait(barrier, n_right + n_col - 2)

    def left_copy(source, i, sem, to):
        return pltpu.make_async_remote_copy(
            src_ref=left.at[source, i],
            dst_ref=left.at[source, i],
            send_sem=sem.at[source, i],
            recv_sem=left_recv.at[source, i],
            device_id={"col": to},
            device_id_type=MESH,
        )

    def own_left_copy(i, sem, to):
        return pltpu.make_async_remote_copy(
            src_ref=x_ref.at[i],
            dst_ref=left.at[c, i],
            send_sem=sem.at[c, i],
            recv_sem=left_recv.at[c, i],
            device_id={"col": to},
            device_id_type=MESH,
        )

    def right_copy(step):
        return pltpu.make_async_remote_copy(
            src_ref=x_ref,
            dst_ref=right_view(me),
            send_sem=right_send.at[step],
            recv_sem=right_recv.at[r],
            device_id={"row": lax.rem(r + step, n_row)},
            device_id_type=MESH,
        )

    def right_view(who):
        return right.at[pl.ds(who * rows, rows)]

    def core_copy(row, own):
        who = row * n_depth + d
        return pltpu.make_async_remote_copy(
            src_ref=x_ref if own else right_view(who),
            dst_ref=right_view(who),
            send_sem=core_send.at[row],
            recv_sem=core_recv.at[row],
            device_id={"depth": 1 - d},
            device_id_type=MESH,
        )

    def right_names_copy(step, who):
        return pltpu.make_async_remote_copy(
            src_ref=names_ref,
            dst_ref=right_names.at[who],
            send_sem=rn_send.at[step],
            recv_sem=rn_recv.at[who],
            device_id=right_peer(step),
            device_id_type=MESH,
        )

    def left_names_copy(step, who):
        return pltpu.make_async_remote_copy(
            src_ref=names_ref,
            dst_ref=left_names.at[who],
            send_sem=ln_send.at[step],
            recv_sem=ln_recv.at[who],
            device_id={"col": lax.rem(c + step, n_col)},
            device_id_type=MESH,
        )

    for i in range(rows):
        @pl.when(c < n_col - 1)
        def _():
            own_left_copy(i, up_send, c + 1).start()

        @pl.when(c > 0)
        def _():
            own_left_copy(i, down_send, c - 1).start()

    for step in range(1, n_row):
        right_copy(step).start()
    core_copy(r, True).start()
    for step in range(1, n_right):
        right_names_copy(step, me).start()
    for step in range(1, n_col):
        left_names_copy(step, c).start()
    local_right = pltpu.make_async_copy(x_ref, right_view(me), local_sem.at[0])
    local_left = pltpu.make_async_copy(x_ref, left.at[c], local_sem.at[1])
    local_rn = pltpu.make_async_copy(names_ref, right_names.at[me], local_sem.at[2])
    local_ln = pltpu.make_async_copy(names_ref, left_names.at[c], local_sem.at[3])
    for copy in (local_right, local_left, local_rn, local_ln):
        copy.start()
    right[n_right * rows] = jnp.zeros(right.shape[1:], jnp.float32)
    out_ref[...] = jnp.zeros_like(out_ref)
    for copy in (local_right, local_left, local_rn, local_ln):
        copy.wait()
    for step in range(1, n_right):
        right_names_copy(step, lax.rem(me + n_right - step, n_right)).wait_recv()
    for step in range(1, n_col):
        left_names_copy(step, lax.rem(c + n_col - step, n_col)).wait_recv()
    table_right = pltpu.make_async_copy(right_names, right_table, local_sem.at[4])
    table_left = pltpu.make_async_copy(left_names, left_table, local_sem.at[5])
    table_right.start()
    table_left.start()
    table_right.wait()
    table_left.wait()

    def compute(p, i):
        panel_rows = rows * n_depth
        for pair in range(slots // 2):
            first, second = 2 * pair, 2 * pair + 1
            whole = jnp.concatenate([left[p, i, first], left[p, i, second]], axis=1)
            l_high, l_low = split(whole)
            l_both = jnp.concatenate([l_high, l_low], axis=0)
            found = []
            for s in (first, second):
                k = left_table[p, i, s]
                upper = jnp.where(k >= rows, 1, 0)
                who, inside = p * n_depth + upper, k - upper * rows
                names = [right_table[who, inside, t] for t in range(slots)]
                base = p * panel_rows + k
                found.append((base, names))
            for half in range(slots // 2):
                cols = []
                for u in (2 * half, 2 * half + 1):
                    want = kept_ref[i, u]
                    parts = []
                    for base, names in found:
                        row, slot = n_right * rows, 0
                        for t in range(slots):
                            hit = names[t] == want
                            row = jnp.where(hit, base, row)
                            slot = jnp.where(hit, t, slot)
                        parts.append(right[row, slot])
                    cols.append(jnp.concatenate(parts, axis=0))
                r_high, r_low = split(jnp.concatenate(cols, axis=1))
                both = jnp.dot(l_both, r_high, preferred_element_type=jnp.float32)
                half_rows = whole.shape[0]
                total = both[:half_rows] + both[half_rows:]
                total += jnp.dot(l_high, r_low, preferred_element_type=jnp.float32)
                width = whole.shape[0]
                out_ref[i, 2 * half] += total[:, :width]
                out_ref[i, 2 * half + 1] += total[:, width:]

    def compute_panel(p):
        def one(i, carry):
            compute(p, i)
            return carry

        lax.fori_loop(0, rows, one, 0)

    for dist in range(1, n_col - 1):
        for i in range(rows):
            @pl.when(c - dist >= 0)
            def _():
                left_copy(c - dist, i, up_send, c).wait_recv()

                @pl.when(c < n_col - 1)
                def _():
                    left_copy(c - dist, i, up_send, c + 1).start()

            @pl.when(c + dist < n_col)
            def _():
                left_copy(c + dist, i, down_send, c).wait_recv()

                @pl.when(c > 0)
                def _():
                    left_copy(c + dist, i, down_send, c - 1).start()

    for step in range(1, n_row):
        source = lax.rem(r + n_row - step, n_row)
        pltpu.make_async_remote_copy(
            src_ref=x_ref,
            dst_ref=right_view(source * n_depth + d),
            send_sem=right_send.at[step],
            recv_sem=right_recv.at[source],
            device_id={"row": source},
            device_id_type=MESH,
        ).wait_recv()
        core_copy(source, False).start()
    for row in range(n_row):
        other = row * n_depth + 1 - d
        pltpu.make_async_remote_copy(
            src_ref=x_ref,
            dst_ref=right_view(other),
            send_sem=core_send.at[row],
            recv_sem=core_recv.at[row],
            device_id={"depth": 1 - d},
            device_id_type=MESH,
        ).wait_recv()

    compute_panel(c)
    for dist in range(1, n_col - 1):
        @pl.when(c - dist >= 0)
        def _():
            compute_panel(c - dist)

        @pl.when(c + dist < n_col)
        def _():
            compute_panel(c + dist)

    last = n_col - 1

    def finish(source, sem):
        def one(i, carry):
            left_copy(source, i, sem, c).wait_recv()
            compute(source, i)
            return carry

        lax.fori_loop(0, rows, one, 0)

    @pl.when(c == last)
    def _():
        finish(c - last, up_send)

    @pl.when(c == 0)
    def _():
        finish(c + last, down_send)

    for step in range(1, n_row):
        right_copy(step).wait_send()
    core_copy(r, True).wait_send()
    for step in range(1, n_row):
        core_copy(lax.rem(r + step, n_row), False).wait_send()
    for step in range(1, n_right):
        right_names_copy(step, me).wait_send()
    for step in range(1, n_col):
        left_names_copy(step, c).wait_send()

    def drain(i, carry):
        @pl.when(c < n_col - 1)
        def _():
            own_left_copy(i, up_send, c + 1).wait_send()
            for dist in range(1, n_col - 1):
                @pl.when(c - dist >= 0)
                def _():
                    left_copy(c - dist, i, up_send, c + 1).wait_send()

        @pl.when(c > 0)
        def _():
            own_left_copy(i, down_send, c - 1).wait_send()
            for dist in range(1, n_col - 1):
                @pl.when(c + dist < n_col)
                def _():
                    left_copy(c + dist, i, down_send, c - 1).wait_send()

        return carry

    lax.fori_loop(0, rows, drain, 0)


def per_device(sizes, x_blocks, x_cols, c_cols):
    n_row, n_col, n_depth = sizes
    rows, slots, size, _ = x_blocks.shape
    n_right = n_row * n_depth
    names = jnp.pad(x_cols, ((0, -rows % 8), (0, 128 - slots)))
    dma = pltpu.SemaphoreType.DMA
    return pl.pallas_call(
        functools.partial(kernel, sizes),
        out_shape=jax.ShapeDtypeStruct((rows, c_cols.shape[1], size, size), jnp.float32),
        in_specs=[
            pl.BlockSpec(memory_space=pltpu.SMEM),
            pl.BlockSpec(memory_space=pltpu.VMEM),
            pl.BlockSpec(memory_space=pltpu.VMEM),
        ],
        out_specs=pl.BlockSpec(memory_space=pltpu.VMEM),
        scratch_shapes=[
            pltpu.VMEM((n_right * rows + 1, slots, size, size), jnp.float32),
            pltpu.VMEM((n_col, rows, slots, size, size), jnp.float32),
            pltpu.VMEM((n_right,) + names.shape, jnp.int32),
            pltpu.VMEM((n_col,) + names.shape, jnp.int32),
            pltpu.SMEM((n_right,) + names.shape, jnp.int32),
            pltpu.SMEM((n_col,) + names.shape, jnp.int32),
            dma((n_row,)),
            dma((n_row,)),
            dma((n_row,)),
            dma((n_row,)),
            dma((n_col, rows)),
            dma((n_col, rows)),
            dma((n_col, rows)),
            dma((n_right,)),
            dma((n_right,)),
            dma((n_col,)),
            dma((n_col,)),
            dma((6,)),
        ],
        compiler_params=pltpu.CompilerParams(
            collective_id=0, has_side_effects=True, vmem_limit_bytes=56 * 1024 * 1024
        ),
    )(c_cols, names, x_blocks)


def solution(mesh):
    sizes = (mesh.shape["row"], mesh.shape["col"], mesh.shape["depth"])
    return jax.shard_map(
        functools.partial(per_device, sizes),
        mesh=mesh,
        in_specs=(
            P(("row", "depth"), "col", None, None),
            P(("row", "depth"), "col"),
            P(("row", "depth"), "col"),
        ),
        out_specs=P(("row", "depth"), "col", None, None),
        check_vma=False,
    )
```

```python
import functools

import jax
import jax.numpy as jnp
from jax import lax
from jax.experimental import pallas as pl
from jax.experimental.pallas import tpu as pltpu
from jax.sharding import PartitionSpec as P

MESH = pl.DeviceIdType.MESH


def split(value):
    high = value.astype(jnp.bfloat16)
    low = (value - high.astype(jnp.float32)).astype(jnp.bfloat16)
    return high, low


def kernel(
    sizes,
    names_ref,
    x_ref,
    out_ref,
    right,
    left,
    right_names,
    left_names,
    right_table,
    left_table,
    own_send,
    pass_send,
    right_recv,
    core_send,
    core_recv,
    up_send,
    down_send,
    left_recv,
    rn_send,
    rn_recv,
    ln_send,
    ln_recv,
    local_sem,
):
    n_row, n_col, n_depth = sizes
    rows, slots = x_ref.shape[0], x_ref.shape[1]
    n_right = n_row * n_depth
    n_group = n_row // 2
    r, c, d = lax.axis_index("row"), lax.axis_index("col"), lax.axis_index("depth")
    me = r * n_depth + d
    group, parity = r // 2, lax.rem(r, 2)
    pair = group * 2 + 1 - parity

    def right_peer(step):
        other = lax.rem(me + step, n_right)
        return {"row": other // n_depth, "depth": lax.rem(other, n_depth)}

    barrier = pltpu.get_barrier_semaphore()
    for step in range(1, n_right):
        pl.semaphore_signal(barrier, inc=1, device_id=right_peer(step), device_id_type=MESH)
    for step in range(1, n_col):
        pl.semaphore_signal(
            barrier, inc=1, device_id={"col": lax.rem(c + step, n_col)}, device_id_type=MESH
        )
    pl.semaphore_wait(barrier, n_right + n_col - 2)

    def remote(src, dst, send, recv, to):
        return pltpu.make_async_remote_copy(
            src_ref=src, dst_ref=dst, send_sem=send, recv_sem=recv, device_id=to, device_id_type=MESH
        )

    def left_copy(source, i, sem, to, own=False):
        return remote(
            x_ref.at[i] if own else left.at[source, i],
            left.at[source, i],
            sem.at[source, i],
            left_recv.at[source, i],
            {"col": to},
        )

    def block_row(row, depth, i):
        return (row * n_depth + depth) * rows + i

    def right_copy(row, i, step, own):
        to = pair if step == 0 else lax.rem(group + step, n_group) * 2 + parity
        at = right.at[block_row(row, d, i)]
        sem = own_send if own else pass_send
        return remote(
            x_ref.at[i] if own else at, at, sem.at[step, i], right_recv.at[row, i], {"row": to}
        )

    def core_copy(row, depth, i, own=False):
        at = right.at[block_row(row, depth, i)]
        return remote(
            x_ref.at[i] if own else at, at, core_send.at[row, i], core_recv.at[row, i], {"depth": 1 - d}
        )

    def right_names_copy(step, who):
        return remote(names_ref, right_names.at[who], rn_send.at[step], rn_recv.at[who], right_peer(step))

    def left_names_copy(step, who):
        return remote(
            names_ref, left_names.at[who], ln_send.at[step], ln_recv.at[who], {"col": lax.rem(c + step, n_col)}
        )

    for step in range(1, n_right):
        right_names_copy(step, me).start()
    for step in range(1, n_col):
        left_names_copy(step, c).start()
    for i in range(rows):
        @pl.when(c < n_col - 1)
        def _():
            left_copy(c, i, up_send, c + 1, True).start()

        @pl.when(c > 0)
        def _():
            left_copy(c, i, down_send, c - 1, True).start()

        for step in range(n_group):
            right_copy(r, i, step, True).start()
    local_right = pltpu.make_async_copy(x_ref, right.at[pl.ds(me * rows, rows)], local_sem.at[0])
    local_left = pltpu.make_async_copy(x_ref, left.at[c], local_sem.at[1])
    local_rn = pltpu.make_async_copy(names_ref, right_names.at[me], local_sem.at[2])
    local_ln = pltpu.make_async_copy(names_ref, left_names.at[c], local_sem.at[3])
    for copy in (local_rn, local_ln, local_right, local_left):
        copy.start()
    for i in range(rows):
        core_copy(r, d, i, True).start()
    right[n_right * rows] = jnp.zeros(right.shape[1:], jnp.float32)
    out_ref[...] = jnp.zeros_like(out_ref)
    for copy in (local_right, local_left, local_rn, local_ln):
        copy.wait()

    def compute(p, i):
        panel_rows = rows * n_depth
        for pair in range(slots // 2):
            first, second = 2 * pair, 2 * pair + 1
            whole = jnp.concatenate([left[p, i, first], left[p, i, second]], axis=1)
            l_high, l_low = split(whole)
            l_both = jnp.concatenate([l_high, l_low], axis=0)
            found = []
            for s in (first, second):
                k = left_table[p, i, s]
                upper = jnp.where(k >= rows, 1, 0)
                who, inside = p * n_depth + upper, k - upper * rows
                names = [right_table[who, inside, t] for t in range(slots)]
                base = p * panel_rows + k
                found.append((base, names))
            for half in range(slots // 2):
                cols = []
                for u in (2 * half, 2 * half + 1):
                    want = right_table[me, i, slots + u]
                    parts = []
                    for base, names in found:
                        row, slot = n_right * rows, 0
                        for t in range(slots):
                            hit = names[t] == want
                            row = jnp.where(hit, base, row)
                            slot = jnp.where(hit, t, slot)
                        parts.append(right[row, slot])
                    cols.append(jnp.concatenate(parts, axis=0))
                r_high, r_low = split(jnp.concatenate(cols, axis=1))
                both = jnp.dot(l_both, r_high, preferred_element_type=jnp.float32)
                half_rows = whole.shape[0]
                total = both[:half_rows] + both[half_rows:]
                total += jnp.dot(l_high, r_low, preferred_element_type=jnp.float32)
                width = whole.shape[0]
                out_ref[i, 2 * half] += total[:, :width]
                out_ref[i, 2 * half + 1] += total[:, width:]

    def compute_panel(p):
        def one(i, carry):
            compute(p, i)
            return carry

        lax.fori_loop(0, rows, one, 0)

    def pass_left(dist, i):
        @pl.when(c - dist >= 0)
        def _():
            left_copy(c - dist, i, up_send, c).wait_recv()

            @pl.when(c < n_col - 1)
            def _():
                left_copy(c - dist, i, up_send, c + 1).start()

        @pl.when(c + dist < n_col)
        def _():
            left_copy(c + dist, i, down_send, c).wait_recv()

            @pl.when(c > 0)
            def _():
                left_copy(c + dist, i, down_send, c - 1).start()

    for i in range(rows):
        pass_left(1, i)
        right_copy(pair, i, 0, True).wait_recv()
        for step in range(1, n_group):
            right_copy(pair, i, step, False).start()
        core_copy(pair, d, i).start()
    for step in range(1, n_group):
        there = lax.rem(group + n_group - step, n_group) * 2
        for i in range(rows):
            right_copy(there + parity, i, step, True).wait_recv()
            core_copy(there + parity, d, i).start()
        for i in range(rows):
            if step == 1:
                pass_left(2, i)
            right_copy(there + 1 - parity, i, step, False).wait_recv()
            core_copy(there + 1 - parity, d, i).start()
    for dist in range(3, n_col - 1):
        for i in range(rows):
            pass_left(dist, i)

    for step in range(1, n_right):
        right_names_copy(step, lax.rem(me + n_right - step, n_right)).wait_recv()
    for step in range(1, n_col):
        left_names_copy(step, lax.rem(c + n_col - step, n_col)).wait_recv()
    table_right = pltpu.make_async_copy(right_names, right_table, local_sem.at[4])
    table_left = pltpu.make_async_copy(left_names, left_table, local_sem.at[5])
    table_right.start()
    table_left.start()
    table_right.wait()
    table_left.wait()
    for row in range(n_row):
        for i in range(rows):
            core_copy(row, 1 - d, i).wait_recv()

    compute_panel(c)
    for dist in range(1, n_col - 1):
        @pl.when(c - dist >= 0)
        def _():
            compute_panel(c - dist)

        @pl.when(c + dist < n_col)
        def _():
            compute_panel(c + dist)

    last = n_col - 1

    def finish(source, sem):
        def one(i, carry):
            left_copy(source, i, sem, c).wait_recv()
            compute(source, i)
            return carry

        lax.fori_loop(0, rows, one, 0)

    @pl.when(c == last)
    def _():
        finish(c - last, up_send)

    @pl.when(c == 0)
    def _():
        finish(c + last, down_send)

    for step in range(1, n_right):
        right_names_copy(step, me).wait_send()
    for step in range(1, n_col):
        left_names_copy(step, c).wait_send()

    def drain(i, carry):
        for step in range(n_group):
            right_copy(r, i, step, True).wait_send()
        for step in range(1, n_group):
            right_copy(pair, i, step, False).wait_send()
        for row in range(n_row):
            core_copy(row, d, i).wait_send()

        @pl.when(c < n_col - 1)
        def _():
            left_copy(c, i, up_send, c + 1).wait_send()
            for dist in range(1, n_col - 1):
                @pl.when(c - dist >= 0)
                def _():
                    left_copy(c - dist, i, up_send, c + 1).wait_send()

        @pl.when(c > 0)
        def _():
            left_copy(c, i, down_send, c - 1).wait_send()
            for dist in range(1, n_col - 1):
                @pl.when(c + dist < n_col)
                def _():
                    left_copy(c + dist, i, down_send, c - 1).wait_send()

        return carry

    lax.fori_loop(0, rows, drain, 0)


def per_device(sizes, x_blocks, x_cols, c_cols):
    n_row, n_col, n_depth = sizes
    rows, slots, size, _ = x_blocks.shape
    n_right = n_row * n_depth
    kept = c_cols.shape[1]
    names = jnp.concatenate([x_cols, c_cols], axis=1)
    names = jnp.pad(names, ((0, -rows % 8), (0, 128 - slots - kept)))
    dma = pltpu.SemaphoreType.DMA
    return pl.pallas_call(
        functools.partial(kernel, sizes),
        out_shape=jax.ShapeDtypeStruct((rows, kept, size, size), jnp.float32),
        in_specs=[
            pl.BlockSpec(memory_space=pltpu.VMEM),
            pl.BlockSpec(memory_space=pl.ANY),
        ],
        out_specs=pl.BlockSpec(memory_space=pltpu.VMEM),
        scratch_shapes=[
            pltpu.VMEM((n_right * rows + 1, slots, size, size), jnp.float32),
            pltpu.VMEM((n_col, rows, slots, size, size), jnp.float32),
            pltpu.VMEM((n_right,) + names.shape, jnp.int32),
            pltpu.VMEM((n_col,) + names.shape, jnp.int32),
            pltpu.SMEM((n_right,) + names.shape, jnp.int32),
            pltpu.SMEM((n_col,) + names.shape, jnp.int32),
            dma((n_row // 2, rows)),
            dma((n_row // 2, rows)),
            dma((n_row, rows)),
            dma((n_row, rows)),
            dma((n_row, rows)),
            dma((n_col, rows)),
            dma((n_col, rows)),
            dma((n_col, rows)),
            dma((n_right,)),
            dma((n_right,)),
            dma((n_col,)),
            dma((n_col,)),
            dma((6,)),
        ],
        compiler_params=pltpu.CompilerParams(
            collective_id=0, has_side_effects=True, vmem_limit_bytes=56 * 1024 * 1024
        ),
    )(names, x_blocks)


def solution(mesh):
    sizes = (mesh.shape["row"], mesh.shape["col"], mesh.shape["depth"])
    return jax.shard_map(
        functools.partial(per_device, sizes),
        mesh=mesh,
        in_specs=(
            P(("row", "depth"), "col", None, None),
            P(("row", "depth"), "col"),
            P(("row", "depth"), "col"),
        ),
        out_specs=P(("row", "depth"), "col", None, None),
        check_vma=False,
    )
```
